32 devices in a mesh: px: 4 (over x, core), py: 8 (over z, y).
Axes of the slice: x: 2, y: 2, z: 4, core: 2. Of those that a mesh axis runs over, the one named last changes fastest.
Arguments:
- displacement: float32 [6, 64, 1024], P(None, 'px', 'py'), may hold values from -4 to 4
- velocity: float32 [6, 64, 1024], P(None, 'px', 'py'), may hold values from -6 to 6
- load: float32 [6, 64, 1024], P(None, 'px', 'py'), may hold values from -24 to 24
- inv_mass: float32 [6, 64, 1024], P(None, 'px', 'py'), may hold values from 0.2 to 1
- history: float32 [128, 64, 1024], P(None, 'px', 'py'), may hold values from -6 to 6
- contact_home: float32 [128, 64, 1024], P(None, 'px', 'py'), may hold values from 0.25 to 4
- recv_contact: float32 [4, 8, 128, 1216], P('px', 'py'), may hold values from 0.25 to 4
- stiff_base: float32 [24, 24], replicated, as said below
- strain_map: float32 [128, 24], replicated, may hold values from -1.25 to 1.25
- slot_table: int32 [4, 8, 1216], P('px', 'py'), may hold values from 0 to 2048, as said below
Outputs:
- springback: float32 [6, 64, 1024], P(None, 'px', 'py')
- velocity_out: float32 [6, 64, 1024], P(None, 'px', 'py')
- history_out: float32 [128, 64, 1024], P(None, 'px', 'py')
- residual: float32 [6, 64, 1024], P(None, 'px', 'py')
The draws below stay inside these ranges and needn't reach their ends.
Inputs may be any that keep to these rules, and one draw needn't show every extreme that they name: `slot_table`: for each source block and destination device d, the slots d * 38 .. d * 38 + 37 hold distinct local shell indices first and then 16 * 128; no shell appears twice in one source block; no block sends to itself; every source block fills all 38 slots toward some destination, and about half of the source blocks fill all slots toward every other device. `stiff_base`: Symmetric, with diagonal entries of 5 to 7 and off-diagonal entries of magnitude at most 0.2.
All inputs are finite; a program needn't handle non-finite values.
Results may differ from the reference program's by a relative error of at most 0.0003.
Values sent between devices are 32-bit elements; how exact they have to be, the bound alone decides.
A program may use at most 128 MiB of HBM per device.

```python
import math
import jax
import jax.numpy as jnp
from jax import lax

CX = 16
CY = 128
HIST = 128
ITERS = 2
CAP = 38
NX = 64
NY = 1024
N_PX = 4
N_PY = 8


def draw_stiff_base(key, part):
    off = jax.random.uniform(key, (24, 24), jnp.float32, -0.1, 0.1)
    sym = off + off.T
    diag = jax.random.uniform(jax.random.fold_in(key, 1), (24,), jnp.float32, 5.0, 7.0)
    eye = jnp.eye(24, dtype=jnp.float32)
    return sym * (1.0 - eye) + eye * diag[None, :]


def draw_slot_table(key, part):
    devices = N_PX * N_PY
    cells = CX * CY

    def one(source):
        inner = jax.random.fold_in(key, source)
        counts = jax.random.randint(jax.random.fold_in(inner, 1), (devices,), 0, CAP + 1)
        heavy = jax.random.randint(jax.random.fold_in(inner, 3), (), 0, 2)
        counts = jnp.where(heavy == 1, CAP, counts)
        dest = jnp.arange(devices)
        counts = jnp.where(dest == (source + 1) % devices, CAP, counts)
        counts = jnp.where(dest == source, 0, counts)
        start = jnp.cumsum(counts) - counts
        order = jax.random.permutation(jax.random.fold_in(inner, 2), cells)
        slot = jnp.arange(CAP)
        position = start[:, None] + slot[None, :]
        live = slot[None, :] < counts[:, None]
        picked = order[jnp.minimum(position, cells - 1)]
        return jnp.where(live, picked, cells).reshape(-1).astype(jnp.int32)
    table = jax.vmap(one)(jnp.arange(devices))
    return table.reshape(N_PX, N_PY, devices * CAP)


def levels(own_key, dims, shards, smallest, high):
    def one(dim, shards_of):
        draws = jax.random.uniform(jax.random.fold_in(jax.random.fold_in(own_key, 6), dim), (shards_of,), jnp.float32, smallest / len(shards), high / len(shards))
        return jnp.repeat(jnp.exp(draws), dims[dim] // shards_of).reshape((-1,) + (1,) * (len(dims) - dim - 1))

    gain = one(*shards[0])
    for cut in shards[1:]:
        gain = gain * one(*cut)
    return gain


def scatter_about(key, extent, spread, reach, pieces=(), kind=jnp.bfloat16):
    values = spread * jax.random.normal(key, extent, jnp.float32)
    if pieces:
        values = values * levels(key, extent, pieces, -0.22, 0.18)
    return jnp.clip(values, -reach, reach).astype(kind)


def setup_inputs(seed: int = 0) -> dict:
    key_of = jax.random.split(jax.random.key(seed), 11)
    displacement = scatter_about(key_of[0], (6, NX, NY), 0.5, 4.0, ((1, 4), (2, 8)), jnp.float32)
    velocity = scatter_about(key_of[1], (6, NX, NY), 1.0, 6.0, ((1, 4), (2, 8)), jnp.float32)
    load = scatter_about(key_of[2], (6, NX, NY), 4.0, 24.0, ((1, 4), (2, 8)), jnp.float32)
    inv_mass = jnp.clip(jnp.exp(math.log(1.0) - 1.609438 * jax.random.uniform(key_of[3], (6, NX, NY), jnp.float32) ** levels(key_of[3], (6, NX, NY), ((1, 4), (2, 8)), -0.2, 0.2)), 0.2, 1.0)
    history = scatter_about(key_of[4], (HIST, NX, NY), 1.0, 6.0, ((1, 4), (2, 8)), jnp.float32)
    contact_home = jnp.clip(jnp.exp(math.log(4.0) - 2.7725887 * jax.random.uniform(key_of[5], (HIST, NX, NY), jnp.float32) ** levels(key_of[5], (HIST, NX, NY), ((1, 4), (2, 8)), -0.2, 0.2)), 0.25, 4.0)
    recv_contact = jnp.clip(jnp.exp(math.log(4.0) - 2.7725887 * jax.random.uniform(key_of[6], (N_PX, N_PY, HIST, N_PX * N_PY * CAP), jnp.float32) ** levels(key_of[6], (N_PX, N_PY, HIST, N_PX * N_PY * CAP), ((0, 4), (1, 8)), -0.2, 0.2)), 0.25, 4.0)
    stiff_base = draw_stiff_base(jax.random.fold_in(key_of[10], 71), 0)
    strain_map = scatter_about(key_of[8], (HIST, 24), 24 ** -0.5, 1.25, (), jnp.float32)
    slot_table = draw_slot_table(jax.random.fold_in(key_of[10], 71), 0)
    return {"displacement": displacement, "velocity": velocity, "load": load, "inv_mass": inv_mass, "history": history, "contact_home": contact_home, "recv_contact": recv_contact, "stiff_base": stiff_base, "strain_map": strain_map, "slot_table": slot_table}


HIGH = lax.Precision.HIGHEST
STEP = 0.2
CORNERS = ((0, 0), (1, 0), (0, 1), (1, 1))


def gather_corners(field):
    rows, cols = field.shape[1], field.shape[2]
    padded = jnp.pad(field, ((0, 0), (0, 1), (0, 1)))
    return jnp.concatenate([padded[:, dx:dx + rows, dy:dy + cols] for dx, dy in CORNERS], axis=0)


def scatter_corners(forces):
    rows, cols = forces.shape[1], forces.shape[2]
    padded = jnp.pad(forces, ((0, 0), (1, 0), (1, 0)))
    total = jnp.zeros((6, rows, cols), jnp.float32)
    for index, (dx, dy) in enumerate(CORNERS):
        total = total + padded[6 * index:6 * index + 6, 1 - dx:1 - dx + rows, 1 - dy:1 - dy + cols]
    return total


def to_blocks(field):
    chans = field.shape[0]
    split = field.reshape(chans, N_PX, CX, N_PY, CY).transpose(1, 3, 0, 2, 4)
    return split.reshape(N_PX * N_PY, chans, CX * CY)


def from_blocks(blocks):
    chans = blocks.shape[1]
    split = blocks.reshape(N_PX, N_PY, chans, CX, CY).transpose(2, 0, 3, 1, 4)
    return split.reshape(chans, N_PX * CX, N_PY * CY)


def reference(displacement, velocity, load, inv_mass, history, contact_home, recv_contact, stiff_base, strain_map, slot_table):
    force_start = scatter_corners(jnp.einsum("ab,bxy->axy", stiff_base, gather_corners(displacement), precision=HIGH))
    velocity_out = velocity + STEP * inv_mass * (load - force_start)
    moved = displacement + STEP * velocity_out
    hist = history.shape[0]
    shells = gather_corners(displacement).reshape(24, -1)
    history_out = history + jnp.dot(strain_map, shells, precision=HIGH).reshape(history.shape)
    devices = N_PX * N_PY
    held = recv_contact.reshape(devices, hist, devices, CAP).transpose(2, 1, 0, 3).reshape(devices, hist, devices * CAP)
    targets = slot_table.reshape(devices, devices * CAP).astype(jnp.int32)
    placed = jax.vmap(lambda block, index, values: block.at[:, index].set(values, mode="drop"))(to_blocks(contact_home), targets, held)
    contact = from_blocks(placed)
    pairs = (strain_map[:, :, None] * strain_map[:, None, :]).reshape(hist, 576)
    weights = (jax.nn.softplus(history_out) * contact).reshape(hist, -1)
    tangent = stiff_base.reshape(576, 1) + jnp.dot(pairs.T, weights, precision=HIGH)
    tangent = tangent.reshape((24, 24) + history.shape[1:])

    def operate(field):
        return scatter_corners(jnp.einsum("abxy,bxy->axy", tangent, gather_corners(field), precision=HIGH))

    rhs = load - force_start
    solution = jnp.zeros_like(rhs)
    residual = rhs
    direction = rhs
    norm_now = jnp.sum(residual * residual)
    for step in range(ITERS):
        image = operate(direction)
        alpha = norm_now / jnp.sum(direction * image)
        solution = solution + alpha * direction
        residual = residual - alpha * image
        if step + 1 < ITERS:
            norm_next = jnp.sum(residual * residual)
            direction = residual + (norm_next / norm_now) * direction
            norm_now = norm_next
    return (moved + solution, velocity_out, history_out, residual)
```

```python
import functools

import jax
import jax.numpy as jnp
from jax import lax
from jax.experimental import pallas as pl
from jax.experimental.pallas import tpu as pltpu
from jax.sharding import PartitionSpec as P

STEP = 0.2
MESH = pl.DeviceIdType.MESH
DIRS = ((1, 0), (-1, 0), (0, 1), (0, -1), (1, 1), (1, -1), (-1, 1), (-1, -1))
F32 = jnp.float32
BF16 = jnp.bfloat16


def up8(n):
    return (n + 7) // 8 * 8


def dot(a, b):
    return jnp.dot(a, b, preferred_element_type=F32)


def dot_t(a, b):
    return lax.dot_general(a, b, (((1,), (1,)), ((), ())), preferred_element_type=F32)


def split(x):
    hi = x.astype(BF16)
    return hi, (x - hi.astype(F32)).astype(BF16)


def kernel(
    npx, npy, cap,
    disp, vel, load, invm, hist_hbm, home_hbm, relaid_hbm, stiff, strain, table,
    spring, velout, hist_out, resid,
    relaid, hist, home, flat, send, recv, onehot, keep, soft, base,
    w1, w2, vm, ve, uf, y, ku, force, part, node, nodex, packed, halo_recv,
    red_send, red_recv,
    in_sem, out_sem, a_send, a_recv, h_send, h_recv, r_send, r_recv,
):
    n = npx * npy
    a = lax.axis_index("px")
    b = lax.axis_index("py")
    me = a * npy + b
    rows, cols = disp.shape[1], disp.shape[2]
    nh = strain.shape[0]
    capp = up8(cap)
    slots = n * capp
    pairs = rows // 2

    relaid_in = pltpu.make_async_copy(relaid_hbm, relaid, in_sem.at[0])
    hist_in = pltpu.make_async_copy(hist_hbm, hist, in_sem.at[1])
    home_in = pltpu.make_async_copy(home_hbm, home, in_sem.at[2])
    relaid_in.start()
    hist_in.start()
    home_in.start()

    def coords(t):
        return (lax.div(t, npy), lax.rem(t, npy))

    halo_recv[...] = jnp.zeros_like(halo_recv)
    recv[me] = jnp.zeros((capp, nh), F32)

    barrier = pltpu.get_barrier_semaphore()

    def greet(k, c):
        pl.semaphore_signal(
            barrier, inc=1, device_id=coords(lax.rem(me + k, n)), device_id_type=MESH
        )
        return c

    lax.fori_loop(1, n, greet, 0)

    lane = lax.broadcasted_iota(jnp.int32, (8, cols), 1)
    lane0 = lane == 0

    def exists(dx, dy):
        return (
            (a + dx >= 0) & (a + dx < npx) & (b + dy >= 0) & (b + dy < npy)
        )

    def halo_copy(e, t, src):
        dx, dy = DIRS[t]
        size = src.shape[0]
        return pltpu.make_async_remote_copy(
            src_ref=src,
            dst_ref=halo_recv.at[e, t, pl.ds(0, size)],
            send_sem=h_send.at[e, t],
            recv_sem=h_recv.at[e, t],
            device_id=(a + dx, b + dy),
            device_id_type=MESH,
        )

    def halo_start(e, items):
        for t, src in items:
            @pl.when(exists(*DIRS[t]))
            def _():
                halo_copy(e, t, src).start()

    def halo_recv_wait(e, items):
        for t, src in items:
            dx, dy = DIRS[t]

            @pl.when(exists(-dx, -dy))
            def _():
                halo_copy(e, t, src).wait_recv()

    def halo_send_wait(e, items):
        for t, src in items:
            @pl.when(exists(*DIRS[t]))
            def _():
                halo_copy(e, t, src).wait_send()

    node[...] = jnp.zeros_like(node)
    vm[...] = jnp.zeros_like(vm)
    for c in range(6):
        vm[0, pl.ds(c, rows, stride=8), :] = disp[c]
        vm[1, pl.ds(c, rows, stride=8), :] = load[c]
    ve[...] = jnp.zeros_like(ve)

    def column(ref, lead, count):
        total = jnp.zeros((8, cols), F32)
        for r in range(count):
            tile = ref[lead, pl.ds(8 * r, 8), :]
            moved = tile if r == 0 else pltpu.roll(tile, r, 1)
            total = jnp.where(lane == r, moved, total)
        return total

    for k in range(2):
        packed[0, 0, pl.ds(8 * k, 8), :] = column(vm, k, rows)
        packed[0, 1, pl.ds(8 * k, 8), :] = vm[k, pl.ds(0, 8), :]

    relaid_in.wait()
    flat[pl.ds(0, n * cap), :] = jnp.transpose(relaid[...])
    for r in range(n * cap, flat.shape[0], 8):
        flat[pl.ds(r, 8), :] = jnp.zeros((8, nh), F32)
    for d in range(n):
        send[d] = flat[pl.ds(d * cap, capp), :]

    pl.semaphore_wait(barrier, n - 1)

    ex0 = [(1, packed.at[0, 1]), (3, packed.at[0, 0]), (7, packed.at[0, 1])]
    halo_start(0, ex0)

    def a2a(target, slot, source):
        return pltpu.make_async_remote_copy(
            src_ref=send.at[slot],
            dst_ref=recv.at[source],
            send_sem=a_send.at[slot],
            recv_sem=a_recv.at[source],
            device_id=coords(target),
            device_id_type=MESH,
        )

    def a2a_start(k, c):
        target = lax.rem(me + k, n)
        a2a(target, target, me).start()
        return c

    lax.fori_loop(1, n, a2a_start, 0)

    def picks(shape, row_dim, shift):
        k = lax.broadcasted_iota(jnp.int32, shape, row_dim)
        m = lax.broadcasted_iota(jnp.int32, shape, 1 - row_dim)
        c = lax.div(k, 6)
        place = 8 * c + (k - 6 * c)
        hit = m == place + shift[0]
        for s in shift[1:]:
            hit = hit | (m == place + s)
        return jnp.where(hit, 1.0, 0.0).astype(BF16)

    sel_hi = picks((24, 96), 0, (0, 32))
    sel_lo = picks((24, 96), 0, (64,))
    sel_rows = picks((32, 24), 1, (0,))
    bh, bl = split(strain[...])
    kh, kl = split(stiff[...])
    kh = dot(sel_rows, kh).astype(BF16)
    kl = dot(sel_rows, kl).astype(BF16)
    w1[pl.ds(0, nh), :] = (dot(bh, sel_hi) + dot(bl, sel_lo)).astype(BF16)
    w1[pl.ds(nh, 32), :] = (dot(kh, sel_hi) + dot(kl, sel_lo)).astype(BF16)
    bth = dot_t(sel_rows, bh).astype(BF16)
    btl = dot_t(sel_rows, bl).astype(BF16)
    w2[...] = jnp.concatenate([bth, bth, btl], axis=1)

    last_row = a == npx - 1
    last_col = b == npy - 1

    def gather(mref, lead, eref):
        def row(r):
            m = mref[lead, pl.ds(8 * r, 8), :]
            e = eref[lead, pl.ds(8 * r, 8), :]
            return m, pltpu.roll(jnp.where(lane0, e, m), cols - 1, 1)

        prev = row(0)
        for p in range(pairs):
            us = []
            for r in (2 * p, 2 * p + 1):
                nxt = row(r + 1)
                u = jnp.concatenate([prev[0], nxt[0], prev[1], nxt[1]], axis=0)
                uf[r] = u
                us.append(u)
                prev = nxt
            u = jnp.concatenate(us, axis=1)
            uh, ul = split(u)
            out = dot(w1[...], jnp.concatenate([uh, ul, uh], axis=0))
            y[p] = out[:nh]
            ku[p] = out[nh:]

    def assemble(e, get):
        below = None
        for r in range(rows + 1):
            main = jnp.zeros((8, cols), F32)
            shift = jnp.zeros((8, cols), F32)
            if r > 0:
                main, shift = below
            if r < rows:
                f = get(r)
                main = main + f[0:8]
                shift = shift + f[16:24]
                below = (f[8:16], f[24:32])
            rolled = pltpu.roll(shift, 1, 1)
            part[e, r, pl.ds(0, 8), :] = main + jnp.where(lane0, 0.0, rolled)
            part[e, r, pl.ds(8, 8), :] = jnp.where(lane0, rolled, 0.0)

    def part_column(e, off):
        total = jnp.zeros((8, cols), F32)
        for r in range(rows + 1):
            tile = part[e, r, pl.ds(off, 8), :]
            moved = tile if r == 0 else pltpu.roll(tile, r, 1)
            total = jnp.where(lane == r, moved, total)
        return total

    def exchange_items(e):
        return [
            (0, part.at[e, rows]),
            (1, part.at[e, 0]),
            (2, packed.at[e + 1, 0, pl.ds(0, 8)]),
            (3, packed.at[e + 1, 0, pl.ds(8, 8)]),
            (4, part.at[e, rows, pl.ds(8, 8)]),
            (5, part.at[e, rows, pl.ds(0, 8)]),
            (6, part.at[e, 0, pl.ds(8, 8)]),
            (7, part.at[e, 0, pl.ds(0, 8)]),
        ]

    def exchange_start(e):
        packed[e + 1, 0, pl.ds(0, 8), :] = part_column(e, 8)
        packed[e + 1, 0, pl.ds(8, 8), :] = part_column(e, 0)
        items = exchange_items(e)
        halo_start(e + 1, items)
        return items

    def got(e, t, off=0):
        return halo_recv[e, t, pl.ds(off, 8), :]

    def at0(x):
        return jnp.where(lane0, x, 0.0)

    def exchange_finish(e, items, put):
        halo_recv_wait(e + 1, items)
        from_prev = got(e + 1, 2)
        from_next = got(e + 1, 3)
        for r in range(rows + 1):
            main = part[e, r, pl.ds(0, 8), :]
            extra = part[e, r, pl.ds(8, 8), :]
            sh = (cols - r) % cols
            pv = from_prev if r == 0 else pltpu.roll(from_prev, sh, 1)
            nx = from_next if r == 0 else pltpu.roll(from_next, sh, 1)
            main = main + at0(pv)
            extra = extra + at0(nx)
            if r == 0:
                main = main + got(e + 1, 0) + at0(got(e + 1, 4))
                extra = extra + got(e + 1, 0, 8) + at0(got(e + 1, 5))
            if r == rows:
                main = main + got(e + 1, 1) + at0(got(e + 1, 6))
                extra = extra + got(e + 1, 1, 8) + at0(got(e + 1, 7))
                main = jnp.where(last_row, 0.0, main)
                extra = jnp.where(last_row, 0.0, extra)
            put(r, main, jnp.where(last_col, 0.0, extra))

    halo_recv_wait(0, ex0)
    for k in range(2):
        vm[k, pl.ds(8 * rows, 8), :] = got(0, 1, 8 * k)
        col = got(0, 3, 8 * k)
        for r in range(rows):
            moved = col if r == 0 else pltpu.roll(col, cols - r, 1)
            ve[k, pl.ds(8 * r, 8), :] = at0(moved)
        ve[k, pl.ds(8 * rows, 8), :] = at0(got(0, 7, 8 * k))

    gather(vm, 0, ve)
    assemble(0, lambda r: ku[r // 2, :, pl.ds(cols * (r % 2), cols)])
    items0 = exchange_start(0)

    hist_in.wait()
    for r in range(rows):
        h = hist[pl.ds(r, nh, stride=rows), :] + y[r // 2, :, pl.ds(cols * (r % 2), cols)]
        hist[pl.ds(r, nh, stride=rows), :] = h
        soft[r // 2, :, pl.ds(cols * (r % 2), cols)] = (
            jnp.maximum(h, 0.0) + jnp.log1p(jnp.exp(-jnp.abs(h)))
        )
    hist_write = pltpu.make_async_copy(hist, hist_out, out_sem.at[0])
    hist_write.start()

    def put_rhs(r, main, extra):
        m = vm[1, pl.ds(8 * r, 8), :] - main
        e = ve[1, pl.ds(8 * r, 8), :] - extra
        node[0, pl.ds(8 * r, 8), :] = m
        nodex[0, pl.ds(8 * r, 8), :] = e

    exchange_finish(0, items0, put_rhs)
    gather(node, 0, nodex)

    rr = jnp.zeros((8, cols), F32)
    for r in range(rows):
        m = node[0, pl.ds(8 * r, 8), :]
        rr = rr + m * m

    for c in range(6):
        r0 = node[0, pl.ds(c, rows, stride=8), :]
        v = vel[c] + STEP * invm[c] * r0
        velout[c] = v
        spring[c] = disp[c] + STEP * v

    place = jnp.broadcast_to(table[...].astype(F32), (nh, n * cap))
    flat[pl.ds(0, n * cap), :] = jnp.transpose(place)
    sub = lax.broadcasted_iota(jnp.int32, (capp, nh), 0)
    lanes = lax.broadcasted_iota(jnp.int32, (capp, nh), 1).astype(F32)
    for d in range(n):
        t = flat[pl.ds(d * cap, capp), :]
        keep[pl.ds(d * capp, capp), :] = jnp.where(
            sub < cap, t - lanes, float(rows * cols)
        )

    ones = jnp.ones((16, slots), BF16)
    home_in.wait()

    def build(p, c):
        for half in range(2):
            lo = (2 * p + half) * cols
            at = lo.astype(F32)
            for s in range(0, slots, 128):
                hit = jnp.where(keep[pl.ds(s, 128), :] == at, 1.0, 0.0)
                onehot[p, pl.ds(s, 128), pl.ds(half * cols, cols)] = hit.astype(BF16)
        mask = dot(ones, onehot[p])[0:1, :]
        stay = 1.0 - mask
        own = jnp.concatenate(
            [home[pl.ds(2 * p + half, nh, stride=rows), :] for half in range(2)], axis=1
        )
        base[p] = soft[p] * own * stay
        return c

    lax.fori_loop(0, pairs, build, 0)

    def a2a_wait(k, c):
        source = lax.rem(me + k, n)
        a2a(me, source, source).wait_recv()
        return c

    lax.fori_loop(1, n, a2a_wait, 0)
    got_all = jnp.transpose(recv[...].reshape(slots, nh))
    ch, cl = split(got_all)
    both = jnp.concatenate([ch, cl], axis=0)

    def push(z, p):
        zh, zl = split(z)
        f = dot(w2[...], jnp.concatenate([zh, zl, zh], axis=0)) + ku[p]
        force[2 * p] = f[:, :cols]
        force[2 * p + 1] = f[:, cols:]

    for p in range(pairs):
        m = dot(both, onehot[p])
        w = base[p] + soft[p] * (m[:nh] + m[nh:])
        base[p] = w
        push(w * y[p], p)

    assemble(1, lambda r: force[r])
    items1 = exchange_start(1)

    def energy():
        total = jnp.zeros((8, cols), F32)
        for r in range(rows):
            prod = uf[r] * force[r]
            total = total + ((prod[0:8] + prod[8:16]) + (prod[16:24] + prod[24:32]))
        return total

    ru = energy()

    def put_u1(r, main, extra):
        node[1, pl.ds(8 * r, 8), :] = main
        nodex[1, pl.ds(8 * r, 8), :] = extra

    exchange_finish(1, items1, put_u1)
    gather(node, 1, nodex)
    uu = jnp.zeros((8, cols), F32)
    for r in range(rows):
        m = node[1, pl.ds(8 * r, 8), :]
        uu = uu + m * m
    for p in range(pairs):
        push(base[p] * y[p], p)
    uv = energy()

    def fold(x):
        return jnp.sum(x, axis=0, keepdims=True)

    zero = jnp.zeros((4, cols), F32)
    mine = jnp.concatenate([fold(rr), fold(ru), fold(uu), fold(uv), zero], axis=0)
    red_send[...] = mine
    red_recv[me] = mine

    def red(target, source):
        return pltpu.make_async_remote_copy(
            src_ref=red_send,
            dst_ref=red_recv.at[source],
            send_sem=r_send.at[target],
            recv_sem=r_recv.at[source],
            device_id=coords(target),
            device_id_type=MESH,
        )

    def red_start(k, c):
        red(lax.rem(me + k, n), me).start()
        return c

    lax.fori_loop(1, n, red_start, 0)

    assemble(2, lambda r: force[r])
    packed[3, 0, pl.ds(0, 8), :] = part_column(2, 8)
    all2 = exchange_items(2)
    items2 = [all2[0], all2[2], all2[4]]
    halo_start(3, items2)
    halo_recv_wait(3, items2)
    from_prev = got(3, 2)
    for r in range(rows):
        main = part[2, r, pl.ds(0, 8), :]
        pv = from_prev if r == 0 else pltpu.roll(from_prev, cols - r, 1)
        main = main + at0(pv)
        if r == 0:
            main = main + got(3, 0) + at0(got(3, 4))
        node[2, pl.ds(8 * r, 8), :] = main

    def red_wait(k, c):
        source = lax.rem(me + k, n)
        red(source, source).wait_recv()
        return c

    lax.fori_loop(1, n, red_wait, 0)
    total = jnp.sum(red_recv[...], axis=0)
    sums = jnp.broadcast_to(jnp.sum(total, axis=1, keepdims=True), (8, cols))
    s_rr, s_ru, s_uu, s_uv = (sums[k : k + 1, :] for k in range(4))
    alpha = s_rr / s_ru
    new = s_rr + alpha * (alpha * s_uu - 2.0 * s_ru)
    grow = 1.0 + new / s_rr
    curve = grow * (grow * s_ru - 2.0 * alpha * s_uu) + alpha * alpha * s_uv
    beta = new / curve
    x_r = alpha + beta * grow
    x_u = -beta * alpha
    r_u = -(alpha + beta * grow)
    r_v = beta * alpha
    for c in range(6):
        r0 = node[0, pl.ds(c, rows, stride=8), :]
        u1 = node[1, pl.ds(c, rows, stride=8), :]
        u2 = node[2, pl.ds(c, rows, stride=8), :]
        spring[c] = spring[c] + x_r * r0 + x_u * u1
        resid[c] = r0 + r_u * u1 + r_v * u2

    hist_write.wait()
    halo_send_wait(0, ex0)
    halo_send_wait(1, items0)
    halo_send_wait(2, items1)
    halo_send_wait(3, items2)

    def drain(k, c):
        target = lax.rem(me + k, n)
        a2a(target, target, me).wait_send()
        red(target, me).wait_send()
        return c

    lax.fori_loop(1, n, drain, 0)


def shards(
    npx, npy,
    displacement, velocity, load, inv_mass, history, contact_home, recv_contact,
    stiff_base, strain_map, slot_table,
):
    nh, rows, cols = history.shape
    n = npx * npy
    width = recv_contact.shape[-1]
    cap = width // n
    capp = up8(cap)
    slots = n * capp
    cells = rows * cols
    pairs = rows // 2
    field = jax.ShapeDtypeStruct(displacement.shape, F32)
    vmem = pl.BlockSpec(memory_space=pltpu.VMEM)
    hbm = pl.BlockSpec(memory_space=pl.ANY)
    nodes = 8 * (rows + 1)
    dma = pltpu.SemaphoreType.DMA
    out = pl.pallas_call(
        functools.partial(kernel, npx, npy, cap),
        out_shape=(field, field, jax.ShapeDtypeStruct((nh * rows, cols), F32), field),
        in_specs=[vmem, vmem, vmem, vmem, hbm, hbm, hbm, vmem, vmem, vmem],
        out_specs=(vmem, vmem, hbm, vmem),
        scratch_shapes=[
            pltpu.VMEM((nh, width), F32),
            pltpu.VMEM((nh * rows, cols), F32),
            pltpu.VMEM((nh * rows, cols), F32),
            pltpu.VMEM((width + capp, nh), F32),
            pltpu.VMEM((n, capp, nh), F32),
            pltpu.VMEM((n, capp, nh), F32),
            pltpu.VMEM((pairs, slots, 2 * cols), BF16),
            pltpu.VMEM((slots, nh), F32),
            pltpu.VMEM((pairs, nh, 2 * cols), F32),
            pltpu.VMEM((pairs, nh, 2 * cols), F32),
            pltpu.VMEM((nh + 32, 96), BF16),
            pltpu.VMEM((32, 3 * nh), BF16),
            pltpu.VMEM((2, nodes, cols), F32),
            pltpu.VMEM((2, nodes, cols), F32),
            pltpu.VMEM((rows, 32, cols), F32),
            pltpu.VMEM((pairs, nh, 2 * cols), F32),
            pltpu.VMEM((pairs, 32, 2 * cols), F32),
            pltpu.VMEM((rows, 32, cols), F32),
            pltpu.VMEM((3, rows + 1, 16, cols), F32),
            pltpu.VMEM((3, nodes, cols), F32),
            pltpu.VMEM((2, nodes, cols), F32),
            pltpu.VMEM((4, 2, 16, cols), F32),
            pltpu.VMEM((4, 8, 16, cols), F32),
            pltpu.VMEM((8, cols), F32),
            pltpu.VMEM((n, 8, cols), F32),
            dma((3,)),
            dma((1,)),
            dma((n,)),
            dma((n,)),
            dma((4, 8)),
            dma((4, 8)),
            dma((n,)),
            dma((n,)),
        ],
        compiler_params=pltpu.CompilerParams(
            collective_id=0, has_side_effects=True, vmem_limit_bytes=48 << 20
        ),
        name="springback",
    )(
        displacement, velocity, load, inv_mass,
        history.reshape(nh * rows, cols), contact_home.reshape(nh * rows, cols),
        recv_contact.reshape(nh, width), stiff_base, strain_map,
        slot_table.reshape(1, width),
    )
    return (out[0], out[1], out[2].reshape(nh, rows, cols), out[3])


def solution(mesh):
    field = P(None, "px", "py")
    return jax.shard_map(
        functools.partial(shards, mesh.shape["px"], mesh.shape["py"]),
        mesh=mesh,
        in_specs=(field,) * 6 + (P("px", "py", None, None), P(), P(), P("px", "py", None)),
        out_specs=(field,) * 4,
        check_vma=False,
    )
```

```python
import functools

import jax
import jax.numpy as jnp
from jax import lax
from jax.experimental import pallas as pl
from jax.experimental.pallas import tpu as pltpu
from jax.sharding import PartitionSpec as P

STEP = 0.2
MESH = pl.DeviceIdType.MESH
DIRS = ((1, 0), (-1, 0), (0, 1), (0, -1), (1, 1), (1, -1), (-1, 1), (-1, -1))
F32 = jnp.float32
BF16 = jnp.bfloat16


def up8(n):
    return (n + 7) // 8 * 8


def dot(a, b):
    return jnp.dot(a, b, preferred_element_type=F32)


def split(x):
    hi = x.astype(BF16)
    return hi, (x - hi.astype(F32)).astype(BF16)


def kernel(
    npx, npy, cap,
    disp_hbm, vel_hbm, load_hbm, invm_hbm, hist_hbm, home_hbm, relaid_hbm, stiff_hbm,
    strain_hbm, table_hbm,
    spring, velout, hist_out, resid,
    disp, vel, load, invm, stiff, strain, table,
    relaid, hist, home, flat, send, recv, onehot, keep, soft, base,
    w1, w2, vm, ve, uf, y, ku, force, part, node, nodex, packed, halo_recv,
    red_send, red_recv,
    in_sem, a_send, a_recv, h_send, h_recv, r_send, r_recv,
):
    n = npx * npy
    a = lax.axis_index("px")
    b = lax.axis_index("py")
    me = a * npy + b
    rows, cols = disp.shape[1], disp.shape[2]
    nh = strain.shape[1]
    capp = up8(cap)
    slots = n * capp
    pairs = rows // 2

    width = n * cap
    relaid_in = pltpu.make_async_copy(
        relaid_hbm, relaid.at[pl.ds(0, width)], in_sem.at[0]
    )
    others = [
        pltpu.make_async_copy(src, dst, in_sem.at[k + 1])
        for k, (src, dst) in enumerate((
            (disp_hbm, disp), (load_hbm, load), (strain_hbm, strain), (stiff_hbm, stiff),
            (hist_hbm, hist), (vel_hbm, vel), (invm_hbm, invm), (table_hbm, table),
            (home_hbm, home),
        ))
    ]
    (disp_in, load_in, strain_in, stiff_in, hist_in, vel_in, invm_in, table_in,
     home_in) = others
    relaid_in.start()
    for copy in others:
        copy.start()

    def coords(t):
        return (lax.div(t, npy), lax.rem(t, npy))

    halo_recv[...] = jnp.zeros_like(halo_recv)
    here = (npy - 1) * npx
    recv[here] = jnp.zeros((capp, nh), F32)

    barrier = pltpu.get_barrier_semaphore()

    def greet(k, c):
        pl.semaphore_signal(
            barrier, inc=1, device_id=coords(lax.rem(me + k, n)), device_id_type=MESH
        )
        return c

    lax.fori_loop(1, n, greet, 0)

    lane = lax.broadcasted_iota(jnp.int32, (8, cols), 1)
    lane0 = lane == 0

    def exists(dx, dy):
        return (
            (a + dx >= 0) & (a + dx < npx) & (b + dy >= 0) & (b + dy < npy)
        )

    def halo_copy(e, t, src):
        dx, dy = DIRS[t]
        size = src.shape[0]
        return pltpu.make_async_remote_copy(
            src_ref=src,
            dst_ref=halo_recv.at[e, t, pl.ds(0, size)],
            send_sem=h_send.at[e, t],
            recv_sem=h_recv.at[e, t],
            device_id=(a + dx, b + dy),
            device_id_type=MESH,
        )

    def halo_start(e, items):
        for t, src in items:
            @pl.when(exists(*DIRS[t]))
            def _():
                halo_copy(e, t, src).start()

    def halo_recv_wait(e, items):
        for t, src in items:
            dx, dy = DIRS[t]

            @pl.when(exists(-dx, -dy))
            def _():
                halo_copy(e, t, src).wait_recv()

    def halo_send_wait(e, items):
        for t, src in items:
            @pl.when(exists(*DIRS[t]))
            def _():
                halo_copy(e, t, src).wait_send()

    node[...] = jnp.zeros_like(node)
    vm[...] = jnp.zeros_like(vm)
    disp_in.wait()
    load_in.wait()
    for c in range(6):
        vm[0, pl.ds(c, rows, stride=8), :] = disp[c]
        vm[1, pl.ds(c, rows, stride=8), :] = load[c]
    ve[...] = jnp.zeros_like(ve)

    def column(ref, lead, count):
        total = jnp.zeros((8, cols), F32)
        for r in range(count):
            tile = ref[lead, pl.ds(8 * r, 8), :]
            moved = tile if r == 0 else pltpu.roll(tile, r, 1)
            total = jnp.where(lane == r, moved, total)
        return total

    for k in range(2):
        packed[0, 0, pl.ds(8 * k, 8), :] = column(vm, k, rows)
        packed[0, 1, pl.ds(8 * k, 8), :] = vm[k, pl.ds(0, 8), :]

    for r in range(width, relaid.shape[0], 8):
        relaid[pl.ds(r, 8), :] = jnp.zeros((8, nh), F32)
    relaid_in.wait()
    for d in range(n):
        send[d] = relaid[pl.ds(d * cap, capp), :]

    pl.semaphore_wait(barrier, n - 1)

    ex0 = [(1, packed.at[0, 1]), (3, packed.at[0, 0]), (7, packed.at[0, 1])]
    halo_start(0, ex0)

    def offset(q):
        r, da = lax.div(q, npx), lax.rem(q, npx)
        odd = lax.rem(r, 2)
        ds = npy // 2 + (1 - 2 * odd) * lax.div(r + 1, 2)
        return da, lax.rem(ds + npy, npy)

    def a2a(q):
        da, ds = offset(q)
        ta, tb = lax.rem(a + da, npx), lax.rem(b + ds, npy)
        return pltpu.make_async_remote_copy(
            src_ref=send.at[ta * npy + tb],
            dst_ref=recv.at[q],
            send_sem=a_send.at[q],
            recv_sem=a_recv.at[q],
            device_id=(ta, tb),
            device_id_type=MESH,
        )

    def source_of(q):
        da, ds = offset(q)
        return lax.rem(a - da + npx, npx) * npy + lax.rem(b - ds + npy, npy)

    def a2a_start(q, c):
        a2a(q).start()
        return c

    def each(lo, hi, body):
        if lo < min(hi, here):
            lax.fori_loop(lo, min(hi, here), body, 0)
        if max(lo, here + 1) < hi:
            lax.fori_loop(max(lo, here + 1), hi, body, 0)

    each(0, n, a2a_start)

    def picks(shape, row_dim, shift):
        k = lax.broadcasted_iota(jnp.int32, shape, row_dim)
        m = lax.broadcasted_iota(jnp.int32, shape, 1 - row_dim)
        c = lax.div(k, 6)
        place = 8 * c + (k - 6 * c)
        hit = m == place + shift[0]
        for s in shift[1:]:
            hit = hit | (m == place + s)
        return jnp.where(hit, 1.0, 0.0).astype(BF16)

    sel_hi = picks((24, 96), 0, (0, 32))
    sel_lo = picks((24, 96), 0, (64,))
    sel_rows = picks((32, 24), 1, (0,))
    strain_in.wait()
    stiff_in.wait()
    bth, btl = split(strain[...])
    bh, bl = split(jnp.transpose(strain[...]))
    kh, kl = split(stiff[...])
    kh = dot(sel_rows, kh).astype(BF16)
    kl = dot(sel_rows, kl).astype(BF16)
    w1[pl.ds(0, nh), :] = (dot(bh, sel_hi) + dot(bl, sel_lo)).astype(BF16)
    w1[pl.ds(nh, 32), :] = (dot(kh, sel_hi) + dot(kl, sel_lo)).astype(BF16)
    bth = dot(sel_rows, bth).astype(BF16)
    btl = dot(sel_rows, btl).astype(BF16)
    w2[...] = jnp.concatenate([bth, bth, btl], axis=1)

    last_row = a == npx - 1
    last_col = b == npy - 1

    def gather(mref, lead, eref):
        def row(r):
            m = mref[lead, pl.ds(8 * r, 8), :]
            e = eref[lead, pl.ds(8 * r, 8), :]
            return m, pltpu.roll(jnp.where(lane0, e, m), cols - 1, 1)

        prev = row(0)
        for p in range(pairs):
            us = []
            for r in (2 * p, 2 * p + 1):
                nxt = row(r + 1)
                u = jnp.concatenate([prev[0], nxt[0], prev[1], nxt[1]], axis=0)
                uf[r] = u
                us.append(u)
                prev = nxt
            u = jnp.concatenate(us, axis=1)
            uh, ul = split(u)
            out = dot(w1[...], jnp.concatenate([uh, ul, uh], axis=0))
            y[p] = out[:nh]
            ku[p] = out[nh:]

    def assemble(e, get):
        below = None
        for r in range(rows + 1):
            main = jnp.zeros((8, cols), F32)
            shift = jnp.zeros((8, cols), F32)
            if r > 0:
                main, shift = below
            if r < rows:
                f = get(r)
                main = main + f[0:8]
                shift = shift + f[16:24]
                below = (f[8:16], f[24:32])
            rolled = pltpu.roll(shift, 1, 1)
            part[e, r, pl.ds(0, 8), :] = main + jnp.where(lane0, 0.0, rolled)
            part[e, r, pl.ds(8, 8), :] = jnp.where(lane0, rolled, 0.0)

    def part_column(e, off):
        total = jnp.zeros((8, cols), F32)
        for r in range(rows + 1):
            tile = part[e, r, pl.ds(off, 8), :]
            moved = tile if r == 0 else pltpu.roll(tile, r, 1)
            total = jnp.where(lane == r, moved, total)
        return total

    def exchange_items(e):
        return [
            (0, part.at[e, rows]),
            (1, part.at[e, 0]),
            (2, packed.at[e + 1, 0, pl.ds(0, 8)]),
            (3, packed.at[e + 1, 0, pl.ds(8, 8)]),
            (4, part.at[e, rows, pl.ds(8, 8)]),
            (5, part.at[e, rows, pl.ds(0, 8)]),
            (6, part.at[e, 0, pl.ds(8, 8)]),
            (7, part.at[e, 0, pl.ds(0, 8)]),
        ]

    def exchange_start(e):
        packed[e + 1, 0, pl.ds(0, 8), :] = part_column(e, 8)
        packed[e + 1, 0, pl.ds(8, 8), :] = part_column(e, 0)
        items = exchange_items(e)
        halo_start(e + 1, items)
        return items

    def got(e, t, off=0):
        return halo_recv[e, t, pl.ds(off, 8), :]

    def at0(x):
        return jnp.where(lane0, x, 0.0)

    def exchange_finish(e, items, put):
        halo_recv_wait(e + 1, items)
        from_prev = got(e + 1, 2)
        from_next = got(e + 1, 3)
        for r in range(rows + 1):
            main = part[e, r, pl.ds(0, 8), :]
            extra = part[e, r, pl.ds(8, 8), :]
            sh = (cols - r) % cols
            pv = from_prev if r == 0 else pltpu.roll(from_prev, sh, 1)
            nx = from_next if r == 0 else pltpu.roll(from_next, sh, 1)
            main = main + at0(pv)
            extra = extra + at0(nx)
            if r == 0:
                main = main + got(e + 1, 0) + at0(got(e + 1, 4))
                extra = extra + got(e + 1, 0, 8) + at0(got(e + 1, 5))
            if r == rows:
                main = main + got(e + 1, 1) + at0(got(e + 1, 6))
                extra = extra + got(e + 1, 1, 8) + at0(got(e + 1, 7))
                main = jnp.where(last_row, 0.0, main)
                extra = jnp.where(last_row, 0.0, extra)
            put(r, main, jnp.where(last_col, 0.0, extra))

    halo_recv_wait(0, ex0)
    for k in range(2):
        vm[k, pl.ds(8 * rows, 8), :] = got(0, 1, 8 * k)
        col = got(0, 3, 8 * k)
        for r in range(rows):
            moved = col if r == 0 else pltpu.roll(col, cols - r, 1)
            ve[k, pl.ds(8 * r, 8), :] = at0(moved)
        ve[k, pl.ds(8 * rows, 8), :] = at0(got(0, 7, 8 * k))

    gather(vm, 0, ve)
    assemble(0, lambda r: ku[r // 2, :, pl.ds(cols * (r % 2), cols)])
    items0 = exchange_start(0)

    hist_in.wait()
    for r in range(rows):
        h = hist[pl.ds(r, nh, stride=rows), :] + y[r // 2, :, pl.ds(cols * (r % 2), cols)]
        hist[pl.ds(r, nh, stride=rows), :] = h
        soft[r // 2, :, pl.ds(cols * (r % 2), cols)] = (
            jnp.maximum(h, 0.0) + jnp.log1p(jnp.exp(-jnp.abs(h)))
        )

    hist_write = pltpu.make_async_copy(hist, hist_out, in_sem.at[10])
    hist_write.start()

    def put_rhs(r, main, extra):
        m = vm[1, pl.ds(8 * r, 8), :] - main
        e = ve[1, pl.ds(8 * r, 8), :] - extra
        node[0, pl.ds(8 * r, 8), :] = m
        nodex[0, pl.ds(8 * r, 8), :] = e

    exchange_finish(0, items0, put_rhs)
    gather(node, 0, nodex)

    rr = jnp.zeros((8, cols), F32)
    for r in range(rows):
        m = node[0, pl.ds(8 * r, 8), :]
        rr = rr + m * m

    vel_in.wait()
    invm_in.wait()
    for c in range(6):
        r0 = node[0, pl.ds(c, rows, stride=8), :]
        v = vel[c] + STEP * invm[c] * r0
        velout[c] = v
        spring[c] = disp[c] + STEP * v

    table_in.wait()
    place = jnp.broadcast_to(table[...].astype(F32), (nh, n * cap))
    flat[pl.ds(0, n * cap), :] = jnp.transpose(place)
    sub = lax.broadcasted_iota(jnp.int32, (capp, nh), 0)
    lanes = lax.broadcasted_iota(jnp.int32, (capp, nh), 1).astype(F32)
    for r in range(n * cap, flat.shape[0], 8):
        flat[pl.ds(r, 8), :] = jnp.zeros((8, nh), F32)

    def arrange(q, c):
        t = flat[pl.ds(source_of(q) * cap, capp), :]
        keep[pl.ds(pl.multiple_of(q * capp, 8), capp), :] = jnp.where(
            sub < cap, t - lanes, float(rows * cols)
        )
        return c

    lax.fori_loop(0, n, arrange, 0)

    ones = jnp.ones((16, slots), BF16)
    home_in.wait()

    def build(p, c):
        for half in range(2):
            lo = (2 * p + half) * cols
            at = lo.astype(F32)
            for s in range(0, slots, 128):
                hit = jnp.where(keep[pl.ds(s, 128), :] == at, 1.0, 0.0)
                onehot[p, pl.ds(s, 128), pl.ds(half * cols, cols)] = hit.astype(BF16)
        mask = dot(ones, onehot[p])[0:1, :]
        stay = 1.0 - mask
        own = jnp.concatenate(
            [home[pl.ds(2 * p + half, nh, stride=rows), :] for half in range(2)], axis=1
        )
        base[p] = soft[p] * own * stay
        return c

    lax.fori_loop(0, pairs, build, 0)

    def a2a_wait(q, c):
        a2a(q).wait_recv()
        return c

    late = n - 2 * nh // capp // 2 * 2

    def arrived(lo, hi):
        each(lo, hi, a2a_wait)
        size = (hi - lo) * capp
        got_all = jnp.transpose(recv[pl.ds(lo, hi - lo)].reshape(size, nh))
        ch, cl = split(got_all)
        return jnp.concatenate([ch, cl], axis=0)

    both = arrived(0, late)
    for p in range(pairs):
        m = dot(both, onehot[p, pl.ds(0, late * capp), :])
        base[p] = base[p] + soft[p] * (m[:nh] + m[nh:])
    both = arrived(late, n)

    def push(z, p):
        zh, zl = split(z)
        f = dot(w2[...], jnp.concatenate([zh, zl, zh], axis=0)) + ku[p]
        force[2 * p] = f[:, :cols]
        force[2 * p + 1] = f[:, cols:]

    for p in range(pairs):
        m = dot(both, onehot[p, pl.ds(late * capp, slots - late * capp), :])
        w = base[p] + soft[p] * (m[:nh] + m[nh:])
        base[p] = w
        push(w * y[p], p)

    assemble(1, lambda r: force[r])
    items1 = exchange_start(1)

    def energy():
        total = jnp.zeros((8, cols), F32)
        for r in range(rows):
            prod = uf[r] * force[r]
            total = total + ((prod[0:8] + prod[8:16]) + (prod[16:24] + prod[24:32]))
        return total

    ru = energy()

    def put_u1(r, main, extra):
        node[1, pl.ds(8 * r, 8), :] = main
        nodex[1, pl.ds(8 * r, 8), :] = extra

    exchange_finish(1, items1, put_u1)
    gather(node, 1, nodex)
    uu = jnp.zeros((8, cols), F32)
    for r in range(rows):
        m = node[1, pl.ds(8 * r, 8), :]
        uu = uu + m * m
    for p in range(pairs):
        push(base[p] * y[p], p)
    uv = energy()

    def fold(x):
        return jnp.sum(x, axis=0, keepdims=True)

    zero = jnp.zeros((4, cols), F32)
    mine = jnp.concatenate([fold(rr), fold(ru), fold(uu), fold(uv), zero], axis=0)
    red_send[...] = mine
    red_recv[me] = mine

    def red(target, source):
        return pltpu.make_async_remote_copy(
            src_ref=red_send,
            dst_ref=red_recv.at[source],
            send_sem=r_send.at[target],
            recv_sem=r_recv.at[source],
            device_id=coords(target),
            device_id_type=MESH,
        )

    def red_start(k, c):
        red(lax.rem(me + k, n), me).start()
        return c

    lax.fori_loop(1, n, red_start, 0)

    assemble(2, lambda r: force[r])
    packed[3, 0, pl.ds(0, 8), :] = part_column(2, 8)
    all2 = exchange_items(2)
    items2 = [all2[0], all2[2], all2[4]]
    halo_start(3, items2)
    halo_recv_wait(3, items2)
    from_prev = got(3, 2)
    for r in range(rows):
        main = part[2, r, pl.ds(0, 8), :]
        pv = from_prev if r == 0 else pltpu.roll(from_prev, cols - r, 1)
        main = main + at0(pv)
        if r == 0:
            main = main + got(3, 0) + at0(got(3, 4))
        node[2, pl.ds(8 * r, 8), :] = main

    def red_wait(k, c):
        source = lax.rem(me + k, n)
        red(source, source).wait_recv()
        return c

    lax.fori_loop(1, n, red_wait, 0)
    total = jnp.sum(red_recv[...], axis=0)
    sums = jnp.broadcast_to(jnp.sum(total, axis=1, keepdims=True), (8, cols))
    s_rr, s_ru, s_uu, s_uv = (sums[k : k + 1, :] for k in range(4))
    alpha = s_rr / s_ru
    new = s_rr + alpha * (alpha * s_uu - 2.0 * s_ru)
    grow = 1.0 + new / s_rr
    curve = grow * (grow * s_ru - 2.0 * alpha * s_uu) + alpha * alpha * s_uv
    beta = new / curve
    x_r = alpha + beta * grow
    x_u = -beta * alpha
    r_u = -(alpha + beta * grow)
    r_v = beta * alpha
    for c in range(6):
        r0 = node[0, pl.ds(c, rows, stride=8), :]
        u1 = node[1, pl.ds(c, rows, stride=8), :]
        u2 = node[2, pl.ds(c, rows, stride=8), :]
        spring[c] = spring[c] + x_r * r0 + x_u * u1
        resid[c] = r0 + r_u * u1 + r_v * u2

    hist_write.wait()
    halo_send_wait(0, ex0)
    halo_send_wait(1, items0)
    halo_send_wait(2, items1)
    halo_send_wait(3, items2)

    def drain(k, c):
        red(lax.rem(me + k, n), me).wait_send()
        return c

    def drain_chunks(q, c):
        a2a(q).wait_send()
        return c

    lax.fori_loop(1, n, drain, 0)
    each(0, n, drain_chunks)


def finish(*refs):
    sem = refs[12]
    steps = []
    for k in range(4):
        length = refs[k].shape[0]
        part = length // 4 if k == 2 else length
        for lo in range(0, length, part):
            at = pl.ds(lo, part)
            m = len(steps)
            steps.append((
                pltpu.make_async_copy(refs[k].at[at], refs[8 + k].at[at], sem.at[0, m]),
                pltpu.make_async_copy(refs[8 + k].at[at], refs[4 + k].at[at], sem.at[1, m]),
            ))
    for fetch, _ in steps:
        fetch.start()
    for fetch, write in steps:
        fetch.wait()
        write.start()
    for _, write in steps:
        write.wait()


def shards(
    npx, npy,
    displacement, velocity, load, inv_mass, history, contact_home, recv_contact,
    stiff_base, strain_map, slot_table,
):
    nh, rows, cols = history.shape
    n = npx * npy
    width = recv_contact.shape[-1]
    cap = width // n
    capp = up8(cap)
    slots = n * capp
    cells = rows * cols
    pairs = rows // 2
    field = jax.ShapeDtypeStruct(displacement.shape, F32)
    vmem = pl.BlockSpec(memory_space=pltpu.VMEM)
    hbm = pl.BlockSpec(memory_space=pltpu.HBM)
    nodes = 8 * (rows + 1)
    dma = pltpu.SemaphoreType.DMA
    out = pl.pallas_call(
        functools.partial(kernel, npx, npy, cap),
        out_shape=(field, field, jax.ShapeDtypeStruct((nh * rows, cols), F32), field),
        in_specs=[hbm] * 10,
        out_specs=(vmem, vmem, hbm, vmem),
        scratch_shapes=[
            pltpu.VMEM(displacement.shape, F32),
            pltpu.VMEM(displacement.shape, F32),
            pltpu.VMEM(displacement.shape, F32),
            pltpu.VMEM(displacement.shape, F32),
            pltpu.VMEM(stiff_base.shape, F32),
            pltpu.VMEM(strain_map.shape[::-1], F32),
            pltpu.VMEM((1, width), jnp.int32),
            pltpu.VMEM((width + capp, nh), F32),
            pltpu.VMEM((nh * rows, cols), F32),
            pltpu.VMEM((nh * rows, cols), F32),
            pltpu.VMEM((width + capp, nh), F32),
            pltpu.VMEM((n, capp, nh), F32),
            pltpu.VMEM((n, capp, nh), F32),
            pltpu.VMEM((pairs, slots, 2 * cols), BF16),
            pltpu.VMEM((slots, nh), F32),
            pltpu.VMEM((pairs, nh, 2 * cols), F32),
            pltpu.VMEM((pairs, nh, 2 * cols), F32),
            pltpu.VMEM((nh + 32, 96), BF16),
            pltpu.VMEM((32, 3 * nh), BF16),
            pltpu.VMEM((2, nodes, cols), F32),
            pltpu.VMEM((2, nodes, cols), F32),
            pltpu.VMEM((rows, 32, cols), F32),
            pltpu.VMEM((pairs, nh, 2 * cols), F32),
            pltpu.VMEM((pairs, 32, 2 * cols), F32),
            pltpu.VMEM((rows, 32, cols), F32),
            pltpu.VMEM((3, rows + 1, 16, cols), F32),
            pltpu.VMEM((3, nodes, cols), F32),
            pltpu.VMEM((2, nodes, cols), F32),
            pltpu.VMEM((4, 2, 16, cols), F32),
            pltpu.VMEM((4, 8, 16, cols), F32),
            pltpu.VMEM((8, cols), F32),
            pltpu.VMEM((n, 8, cols), F32),
            dma((11,)),
            dma((n,)),
            dma((n,)),
            dma((4, 8)),
            dma((4, 8)),
            dma((n,)),
            dma((n,)),
        ],
        compiler_params=pltpu.CompilerParams(
            collective_id=0, has_side_effects=True, vmem_limit_bytes=63 << 20
        ),
        name="springback",
    )(
        displacement, velocity, load, inv_mass,
        history.reshape(nh * rows, cols), contact_home.reshape(nh * rows, cols),
        jnp.swapaxes(recv_contact.reshape(nh, width), 0, 1), stiff_base, strain_map.T,
        slot_table.reshape(1, width),
    )
    out = pl.pallas_call(
        finish,
        out_shape=tuple(jax.ShapeDtypeStruct(x.shape, F32) for x in out),
        in_specs=[hbm] * 4,
        out_specs=(hbm,) * 4,
        scratch_shapes=[pltpu.VMEM(x.shape, F32) for x in out] + [dma((2, 7))],
        compiler_params=pltpu.CompilerParams(vmem_limit_bytes=63 << 20),
        name="finish",
    )(*out)
    return (out[0], out[1], out[2].reshape(nh, rows, cols), out[3])


def solution(mesh):
    field = P(None, "px", "py")
    return jax.shard_map(
        functools.partial(shards, mesh.shape["px"], mesh.shape["py"]),
        mesh=mesh,
        in_specs=(field,) * 6 + (P("px", "py", None, None), P(), P(), P("px", "py", None)),
        out_specs=(field,) * 4,
        check_vma=False,
    )
```
